32 devices in a mesh: seq: 16 (over z, y, x), head: 2 (over core).
Axes of the slice: x: 2, y: 2, z: 4, core: 2. Of those that a mesh axis runs over, the one named last changes fastest.
Arguments:
- queries: bfloat16 [8192, 4096], P('seq', 'head'), may hold values from -6 to 6
- keys: bfloat16 [8192, 4096], P('seq', 'head'), may hold values from -6 to 6
- values: bfloat16 [8192, 4096], P('seq', 'head')
- gain: float32 [4096], P('head'), may hold values from 0.1 to 1.9
- cotangent: bfloat16 [8192, 4096], P('seq', 'head')
- doc_lengths: int32 [16], replicated, may hold values from 1 to 4096, 8192 in all
Outputs:
- attended: bfloat16 [8192, 4096], P('seq', 'head')
- grad_queries: bfloat16 [8192, 4096], P('seq', 'head')
- grad_keys: bfloat16 [8192, 4096], P('seq', 'head')
- grad_values: bfloat16 [8192, 4096], P('seq', 'head')
The draws below stay inside these ranges and needn't reach their ends.
Inputs may be any that keep to these rules, and one draw needn't show every extreme that they name: `doc_lengths`: the lengths sum to 8192; the longest document has exactly 4096 tokens.
All inputs are finite; a program needn't handle non-finite values.
Results may differ from the reference program's by a relative error of at most 0.0059.
Values sent between devices are 32-bit elements; how exact they have to be, the bound alone decides.
A program may use at most 192 MiB of HBM per device.

```python
import math
import jax
import jax.numpy as jnp
import numpy as np
from jax import lax

DH = 128
HEADS = 32
TOK_DEV = 512
D = 4096
LENGTH = 8192
DOC_MAX = 4096
DOCS = 16


def draw_values(key, part):
    key = jax.random.fold_in(key, 11)
    k_noise, k_column, k_row = jax.random.split(key, 3)
    column_ramp = jnp.arange(D, dtype=jnp.float32) / D
    column_scale = 10.0 ** (0.5 * column_ramp + 0.5 * jax.random.uniform(k_column, (D,), jnp.float32) - 0.5)
    row_scale = 10.0 ** (jax.random.uniform(k_row, (LENGTH, 1), jnp.float32) - 0.5)
    noise_field = jax.random.normal(k_noise, (LENGTH, D), jnp.float32)
    return (noise_field * column_scale * row_scale).astype(jnp.bfloat16)


def draw_cotangent(key, part):
    key = jax.random.fold_in(key, 23)
    k_noise, k_column, k_row = jax.random.split(key, 3)
    column_scale = 10.0 ** (jax.random.uniform(k_column, (D,), jnp.float32) - 0.5)
    row_scale = 10.0 ** (jax.random.uniform(k_row, (LENGTH, 1), jnp.float32) - 0.5)
    noise_field = jax.random.normal(k_noise, (LENGTH, D), jnp.float32)
    return (noise_field * column_scale * row_scale).astype(jnp.bfloat16)


def block_levels(stream_key, shape, pieces, least, largest):
    loudness = 1.0
    for axis_at, parts in pieces:
        draws = jax.random.uniform(jax.random.fold_in(jax.random.fold_in(stream_key, 6), axis_at), (parts,), jnp.float32, least / len(pieces), largest / len(pieces))
        loudness = loudness * jnp.repeat(jnp.exp(draws), shape[axis_at] // parts).reshape((-1,) + (1,) * (len(shape) - 1 - axis_at))
    return loudness


def length_profile(count, total, reach, lean):
    portions = [(1 << 20) // math.isqrt(rank ** lean) + 1 for rank in range(2, count + 1)]
    rest, given = total - reach - (count - 1), [1] * (count - 1)
    while rest > 0:
        candidates = [i for i in range(count - 1) if given[i] < reach]
        mass, budget = sum([portions[i] for i in candidates]), rest
        for i in candidates:
            extra = min(reach - given[i], max(1, budget * portions[i] // mass), rest)
            given[i] = given[i] + extra
            rest = rest - extra
    return np.array([reach] + given)


def ragged_sizes(own_key, number_of, total, most, lean):
    if number_of == 2:
        one = jax.random.randint(own_key, (), max(1, total - most), min(most, total - 1) + 1)
        return jnp.stack([one, total - one])
    lengths = jnp.asarray(length_profile(number_of, total, most, lean), jnp.int32)
    couples = (number_of - 1) // 2
    source_of, sink = lengths[1:1 + 2 * couples:2], lengths[2:2 + 2 * couples:2]
    margin = jnp.minimum(source_of - 1, most - sink)
    shifted = jax.random.randint(jax.random.fold_in(own_key, 1), (couples,), 0, 1 << 20) % (margin + 1)
    lengths = lengths.at[1:1 + 2 * couples:2].set(source_of - shifted).at[2:2 + 2 * couples:2].set(sink + shifted)
    return lengths[jax.random.permutation(jax.random.fold_in(own_key, 2), number_of)]


def centred(rng, extent, scale, bound, pieces=(), held_as=jnp.bfloat16):
    factor_of = block_levels(rng, extent, pieces, -0.22, 0.18) if pieces else 1.0
    result = jax.random.normal(rng, extent, jnp.float32) * scale * factor_of
    return jnp.minimum(jnp.maximum(result, -bound), bound).astype(held_as)


def setup_inputs(seed: int = 0) -> dict:
    key_list = jax.random.split(jax.random.key(seed), 7)
    return {
        "queries": centred(key_list[0], (LENGTH, D), 1.0, 6.0, ((0, 16), (1, 2))),
        "keys": centred(key_list[1], (LENGTH, D), 1.0, 6.0, ((0, 16), (1, 2))),
        "values": draw_values(jax.random.fold_in(key_list[6], 71), 0),
        "gain": jnp.clip(1.0 + 0.18 * jax.random.normal(key_list[3], (D,), jnp.float32), 0.1, 1.9),
        "cotangent": draw_cotangent(jax.random.fold_in(key_list[6], 71), 0),
        "doc_lengths": ragged_sizes(key_list[5], DOCS, LENGTH, DOC_MAX, 2).astype(jnp.int32),
    }


epsilon = 1e-05

def doc_index(starts, positions):
    return lax.optimization_barrier(jnp.sum((starts[None, :] <= positions[:, None]).astype(jnp.int32), axis=1)).astype(jnp.int32)

def rounded(array):
    return lax.optimization_barrier(array.astype(jnp.bfloat16)).astype(jnp.float32)

def block_masks(doc_ids, edge_docs):
    offsets = jnp.arange(TOK_DEV, dtype=jnp.int32)
    visible = (doc_ids[:, None] == doc_ids[None, :]) & (offsets[:, None] >= offsets[None, :])
    entering_state = (doc_ids == edge_docs[0])[:, None, None]
    opening_boundary = (doc_ids == edge_docs[1])[:, None, None]
    closing_boundary = (doc_ids == edge_docs[2])[:, None, None]
    leaving_state = (doc_ids == edge_docs[3])[:, None, None]
    return (visible, entering_state, opening_boundary, closing_boundary, leaving_state)

def reference(queries, keys, values, gain, cotangent, doc_lengths):
    blocks = LENGTH // TOK_DEV
    model_width = HEADS * DH
    starts = (jnp.cumsum(doc_lengths) - doc_lengths).astype(jnp.int32)
    positions = jnp.arange(LENGTH, dtype=jnp.int32)
    doc_ids = doc_index(starts, positions).reshape(blocks, TOK_DEV)
    anchors = jnp.arange(blocks, dtype=jnp.int32) * TOK_DEV
    bounds = jnp.stack([anchors - 1, anchors, anchors + TOK_DEV - 1, anchors + TOK_DEV], axis=1).astype(jnp.int32)
    edge_docs = doc_index(starts, bounds.reshape(-1)).reshape(blocks, 4)
    query_blocks = queries.reshape(blocks, TOK_DEV, HEADS, DH)
    key_blocks = keys.reshape(blocks, TOK_DEV, HEADS, DH)
    value_blocks = values.reshape(blocks, TOK_DEV, HEADS, DH)
    grad_blocks = cotangent.reshape(blocks, TOK_DEV, model_width)
    gain_wide = gain.astype(jnp.float32)

    def forward_step(state, inputs):
        query_block, key_block, value_block, grad_block, block_ids, block_edges = inputs
        visible, entering_state, opening_boundary, closing_boundary, leaving_state = block_masks(block_ids, block_edges)
        query_broad = query_block.astype(jnp.float32)
        key_broad = key_block.astype(jnp.float32)
        value_broad = value_block.astype(jnp.float32)
        scores = jnp.einsum('thk,shk->hts', query_broad, key_broad)
        weights = rounded(jnp.where(visible[None], scores, 0.0))
        carried_narrow_state = state.astype(jnp.bfloat16)
        carried_broad_state = lax.optimization_barrier(carried_narrow_state).astype(jnp.float32)
        output_rows = jnp.einsum('hts,shv->thv', weights, value_broad)
        output_rows = output_rows + jnp.where(entering_state, jnp.einsum('ldi,dir->ldr', query_broad, carried_broad_state), 0.0)
        inside_state = jnp.einsum('blp,blq->lpq', jnp.where(closing_boundary, key_broad, 0.0), value_broad)
        keep_forward = (block_edges[2] == block_edges[0]).astype(jnp.float32)
        new_state = inside_state + keep_forward * state
        flat_out = output_rows.reshape(TOK_DEV, model_width)
        scaled_grad = grad_block.astype(jnp.float32) * gain_wide
        root_mean = jnp.sqrt(lax.optimization_barrier(jnp.sum(flat_out * flat_out, axis=1)) / model_width + epsilon)
        attended = (flat_out / root_mean[:, None] * gain_wide).astype(jnp.bfloat16)
        coefficient = lax.optimization_barrier(jnp.sum(scaled_grad * flat_out, axis=1)) / (model_width * root_mean * root_mean)
        grad_out = ((scaled_grad - flat_out * coefficient[:, None]) / root_mean[:, None]).astype(jnp.bfloat16)
        return (new_state, (attended, grad_out, carried_narrow_state))
    zero_state = jnp.zeros((HEADS, DH, DH), jnp.float32)
    forward_inputs = (query_blocks, key_blocks, value_blocks, grad_blocks, doc_ids, edge_docs)
    unused, (attended, grad_outs, carried_lows) = lax.scan(forward_step, zero_state, forward_inputs)

    def backward_step(state, inputs):
        query_block, key_block, value_block, grad_out, carried_narrow_state, block_ids, block_edges = inputs
        visible, entering_state, opening_boundary, closing_boundary, leaving_state = block_masks(block_ids, block_edges)
        query_broad = query_block.astype(jnp.float32)
        key_broad = key_block.astype(jnp.float32)
        value_broad = value_block.astype(jnp.float32)
        gradient_row_list = grad_out.reshape(TOK_DEV, HEADS, DH).astype(jnp.float32)
        carried_broad_state = carried_narrow_state.astype(jnp.float32)
        scores = jnp.einsum('thk,shk->hts', query_broad, key_broad)
        weights = rounded(jnp.where(visible[None], scores, 0.0))
        back_scores = jnp.einsum('thv,shv->hts', gradient_row_list, value_broad)
        back_weights = rounded(jnp.where(visible[None], back_scores, 0.0))
        following_broad = rounded(state)
        gradient_query = jnp.einsum('hts,shk->thk', back_weights, key_broad)
        gradient_query = gradient_query + jnp.where(entering_state, jnp.einsum('esn,son->eso', gradient_row_list, carried_broad_state), 0.0)
        gradient_key = jnp.einsum('hts,thk->shk', back_weights, query_broad)
        gradient_key = gradient_key + jnp.where(leaving_state, jnp.einsum('won,ozn->woz', value_broad, following_broad), 0.0)
        gradient_value = jnp.einsum('hts,thv->shv', weights, gradient_row_list)
        gradient_value = gradient_value + jnp.where(leaving_state, jnp.einsum('xua,uat->xut', key_broad, following_broad), 0.0)
        inside_backward_state = jnp.einsum('dmi,dmc->mic', jnp.where(opening_boundary, query_broad, 0.0), gradient_row_list)
        keep_backward = (block_edges[3] == block_edges[1]).astype(jnp.float32)
        new_state = inside_backward_state + keep_backward * state
        outs = (gradient_query.astype(jnp.bfloat16), gradient_key.astype(jnp.bfloat16), gradient_value.astype(jnp.bfloat16))
        return (new_state, outs)
    backward_inputs = (query_blocks, key_blocks, value_blocks, grad_outs, carried_lows, doc_ids, edge_docs)
    unused_back, (gradient_query, gradient_key, gradient_value) = lax.scan(backward_step, zero_state, backward_inputs, reverse=True)
    shape_out = (LENGTH, model_width)
    return (attended.reshape(shape_out), gradient_query.reshape(shape_out), gradient_key.reshape(shape_out), gradient_value.reshape(shape_out))
```

```python
import functools

import jax
import jax.numpy as jnp
from jax import lax
from jax.experimental import pallas as pl
from jax.experimental.pallas import tpu as pltpu
from jax.sharding import PartitionSpec as P

DH = 128
HEADS = 32
QUAD = 4

epsilon = 1e-05
MESH = pl.DeviceIdType.MESH
F32 = jnp.float32
BF16 = jnp.bfloat16


def nn(a, b):
    return lax.dot_general(a, b, (((1,), (0,)), ((), ())), preferred_element_type=F32)


def nt(a, b):
    return lax.dot_general(a, b, (((1,), (1,)), ((), ())), preferred_element_type=F32)


def tn(a, b):
    return lax.dot_general(a, b, (((0,), (0,)), ((), ())), preferred_element_type=F32)


def pick(flag, one, other):
    return jnp.where(flag, one, other).astype(F32)


def equal(a, b):
    return jnp.where(a == b, 1.0, 0.0).astype(F32)


def kernel(
    n, nh, docs,
    lens, q, k, v, gain, cot,
    att, gq, gk, gv,
    wts, out, gks, grad, carr,
    vis, ment, mopen, mclose, mleave, part, peer,
    loc_f, pair_f, chain_f, rx_f, ry_f, rz_f,
    loc_b, pair_b, chain_b, rx_b, ry_b, rz_b,
    sx_f, sy_f, sz_f, tx_f, ty_f, tz_f,
    sx_b, sy_b, sz_b, tx_b, ty_b, tz_b,
    sh, th,
):
    tokens = q.shape[0]
    half = tokens // 2
    heads = q.shape[1] // DH
    width = float(HEADS * DH)
    me = lax.axis_index("seq")
    mine = lax.axis_index("head")
    odd = lax.rem(me, 2)
    zc = lax.div(me, QUAD)
    nz = n // QUAD
    q0 = zc * QUAD
    upper = lax.div(me - q0, 2)
    pb = me - odd
    px = me + 1 - 2 * odd
    py = me + 2 - 4 * upper
    up = lax.rem(me + QUAD, n)
    down = lax.rem(me + n - QUAD, n)

    barrier = pltpu.get_barrier_semaphore()
    pl.semaphore_signal(barrier, inc=1, device_id={"seq": px}, device_id_type=MESH)
    pl.semaphore_signal(barrier, inc=1, device_id={"seq": py}, device_id_type=MESH)

    @pl.when(zc < nz - 1)
    def _():
        pl.semaphore_signal(barrier, inc=1, device_id={"seq": up}, device_id_type=MESH)

    @pl.when(zc > 0)
    def _():
        pl.semaphore_signal(barrier, inc=1, device_id={"seq": down}, device_id_type=MESH)

    for d in range(1, nh):
        pl.semaphore_signal(
            barrier, inc=1, device_id={"head": lax.rem(mine + d, nh)}, device_id_type=MESH
        )

    starts = []
    total = jnp.int32(0)
    for i in range(docs):
        starts.append(total)
        total = total + lens[i]

    def doc_of(p):
        count = jnp.int32(0)
        for s in starts:
            count = count + jnp.where(s <= p, 1, 0).astype(jnp.int32)
        return count

    before = {}
    after = {}
    for name, i in (("q0", q0), ("q2", q0 + 2), ("q4", q0 + 4), ("pb", pb), ("p1", pb + 1),
                    ("p2", pb + 2), ("me", me), ("m1", me + 1)):
        before[name] = doc_of(i * tokens - 1)
        after[name] = doc_of(i * tokens)

    anchor = me * tokens
    pos_c = lax.broadcasted_iota(jnp.int32, (tokens, DH), 0) + anchor
    doc_c = jnp.zeros((tokens, DH), jnp.int32)
    for s in starts:
        doc_c = doc_c + jnp.where(pos_c >= s, 1, 0)
    ment[...] = jnp.where(doc_c == before["me"], 1.0, 0.0).astype(BF16)
    mopen[...] = jnp.where(doc_c == after["me"], 1.0, 0.0).astype(BF16)
    mclose[...] = jnp.where(doc_c == before["m1"], 1.0, 0.0).astype(BF16)
    mleave[...] = jnp.where(doc_c == after["m1"], 1.0, 0.0).astype(BF16)

    pl.semaphore_wait(
        barrier,
        2 + nh - 1
        + jnp.where(zc < nz - 1, 1, 0).astype(jnp.int32)
        + jnp.where(zc > 0, 1, 0).astype(jnp.int32),
    )

    def cols(h):
        return pl.ds(pl.multiple_of(h * DH, DH), DH)

    def send(src, dst, ss, rs, h, to):
        return pltpu.make_async_remote_copy(
            src_ref=src.at[h], dst_ref=dst.at[h], send_sem=ss.at[h], recv_sem=rs.at[h],
            device_id={"seq": to}, device_id_type=MESH,
        )

    class Scan:
        def __init__(self, bufs, sems, to, place, coef):
            self.loc, self.pair, self.chain, self.rx, self.ry, self.rz = bufs
            self.sx, self.sy, self.sz, self.tx, self.ty, self.tz = sems
            self.to, self.place = to, place
            self.al, self.ar, self.er, self.bl, self.br, self.e2, self.kq, self.e3 = coef

        def cx(self, h):
            return send(self.loc, self.rx, self.sx, self.tx, h, px)

        def cy(self, h):
            return send(self.pair, self.ry, self.sy, self.ty, h, py)

        def cz(self, h):
            return send(self.chain, self.rz, self.sz, self.tz, h, self.to)

        def clear(self):
            @pl.when(self.place == 0)
            def _():
                self.rz[...] = jnp.zeros_like(self.rz)

        def xstage(self, h):
            self.cx(h).wait_recv()
            self.pair[h] = self.al * self.loc[h] + self.ar * self.rx[h]
            self.cy(h).start()

        def ystage(self, h):
            self.cy(h).wait_recv()

            @pl.when(self.place == 0)
            def _():
                self.chain[h] = self.bl * self.pair[h] + self.br * self.ry[h]
                self.cz(h).start()

        def zstage(self, h):
            @pl.when(self.place > 0)
            def _():
                self.cz(h).wait_recv()

            @pl.when((self.place > 0) & (self.place < nz - 1))
            def _():
                total = self.bl * self.pair[h] + self.br * self.ry[h]
                self.chain[h] = total + self.kq * self.rz[h]
                self.cz(h).start()

            return self.er * self.rx[h] + self.e2 * self.ry[h] + self.e3 * self.rz[h]

        def drain(self):
            def body(h, carry):
                self.cx(h).wait_send()
                self.cy(h).wait_send()

                @pl.when(self.place < nz - 1)
                def _():
                    self.cz(h).wait_send()

                return carry

            lax.fori_loop(0, heads, body, 0)

    is_odd, is_upper = odd == 1, upper == 1
    kx = equal(before["p1"], before["p2"])
    ky = equal(before["q2"], before["q4"])
    fwd = Scan(
        (loc_f, pair_f, chain_f, rx_f, ry_f, rz_f),
        (sx_f, sy_f, sz_f, tx_f, ty_f, tz_f),
        up, zc,
        (pick(is_odd, 1.0, kx), pick(is_odd, kx, 1.0), pick(is_odd, 1.0, 0.0),
         pick(is_upper, 1.0, ky), pick(is_upper, ky, 1.0),
         pick(is_upper, equal(before["pb"], before["me"]), 0.0),
         equal(before["q0"], before["q4"]), equal(before["q0"], before["me"])),
    )
    kx = equal(after["pb"], after["p1"])
    ky = equal(after["q0"], after["q2"])
    bwd = Scan(
        (loc_b, pair_b, chain_b, rx_b, ry_b, rz_b),
        (sx_b, sy_b, sz_b, tx_b, ty_b, tz_b),
        down, nz - 1 - zc,
        (pick(is_odd, kx, 1.0), pick(is_odd, 1.0, kx), pick(is_odd, 0.0, 1.0),
         pick(is_upper, ky, 1.0), pick(is_upper, 1.0, ky),
         pick(is_upper, 0.0, equal(after["m1"], after["p2"])),
         equal(after["q0"], after["q4"]), equal(after["m1"], after["q4"])),
    )

    def slots(scan, inside, finish):
        def place_of(s):
            return s - 1 - 2 * scan.place

        def chain_step(s):
            h = place_of(s)

            @pl.when((h >= 0) & (h < heads))
            def _():
                finish(h, scan.zstage(h).astype(BF16))

        def main(s, carry):
            scan.xstage(s)

            @pl.when(s > 0)
            def _():
                scan.ystage(s - 1)

            inside(s)
            chain_step(s)
            return carry

        lax.fori_loop(0, heads, main, 0)
        scan.ystage(heads - 1)

        def tail(s, carry):
            chain_step(s)
            return carry

        lax.fori_loop(heads, heads + 1 + 2 * (nz - 1), tail, 0)

    def first(h, carry):
        c = cols(h)
        loc_f[h] = tn(k[:, c] * mclose[...], v[:, c])
        fwd.cx(h).start()
        return carry

    lax.fori_loop(0, heads, first, 0)
    fwd.clear()
    bwd.clear()

    pos_r = lax.broadcasted_iota(jnp.int32, (8, tokens), 1) + anchor
    doc_r = jnp.zeros((8, tokens), jnp.int32)
    for s in starts:
        doc_r = doc_r + jnp.where(pos_r >= s, 1, 0)
    row = lax.broadcasted_iota(jnp.int32, (tokens, tokens), 0)
    col = lax.broadcasted_iota(jnp.int32, (tokens, tokens), 1)
    vis[...] = jnp.where((doc_c[:, :1] == doc_r[:1, :]) & (row >= col), 1, 0)
    part[...] = jnp.zeros_like(part)

    lo, hi = slice(0, half), slice(half, tokens)

    def masked(scores, rows, columns):
        return jnp.where(vis[rows, columns] != 0, scores, 0.0).astype(BF16)

    def inside_f(h):
        c = cols(h)
        w0 = masked(nt(q[lo, c], k[lo, c]), lo, lo)
        w1 = masked(nt(q[hi, c], k[:, c]), hi, slice(0, tokens))
        wts[h, lo, lo] = w0
        wts[h, hi, :] = w1
        out[lo, c] = nn(w0, v[lo, c])
        out[hi, c] = nn(w1, v[:, c])

    def finish_f(h, low):
        c = cols(h)
        carr[h] = low
        o = out[:, c] + nn(q[:, c] * ment[...], low)
        out[:, c] = o
        part[0] += o * o
        part[1] += (cot[:, c].astype(F32) * gain[:, c]) * o

    slots(fwd, inside_f, finish_f)

    def swap(d):
        return pltpu.make_async_remote_copy(
            src_ref=part, dst_ref=peer.at[d - 1], send_sem=sh.at[d - 1], recv_sem=th.at[d - 1],
            device_id={"head": lax.rem(mine + d, nh)}, device_id_type=MESH,
        )

    for d in range(1, nh):
        swap(d).start()
    for d in range(1, nh):
        swap(d).wait_recv()
    squares, cross = part[0], part[1]
    for d in range(1, nh):
        squares = squares + peer[d - 1, 0]
        cross = cross + peer[d - 1, 1]
    for d in range(1, nh):
        swap(d).wait_send()
    root = jnp.sqrt(jnp.sum(squares, axis=1, keepdims=True) / width + epsilon)
    coef = jnp.sum(cross, axis=1, keepdims=True) / (width * root * root)
    part[0] = jnp.broadcast_to(1.0 / root, (tokens, DH))
    part[1] = jnp.broadcast_to(coef, (tokens, DH))

    def middle(h, carry):
        c = cols(h)
        o = out[:, c]
        inv = part[0]
        gn = gain[:, c]
        att[:, c] = (o * inv * gn).astype(BF16)
        g = ((cot[:, c].astype(F32) * gn - o * part[1]) * inv).astype(BF16)
        grad[:, c] = g
        loc_b[h] = tn(q[:, c] * mopen[...], g)
        bwd.cx(h).start()
        return carry

    lax.fori_loop(0, heads, middle, 0)

    def inside_b(h):
        c = cols(h)
        b0 = masked(nt(grad[lo, c], v[lo, c]), lo, lo)
        b1 = masked(nt(grad[hi, c], v[:, c]), hi, slice(0, tokens))
        entering = nt(grad[:, c] * ment[...], carr[h])
        gq[lo, c] = (nn(b0, k[lo, c]) + entering[lo]).astype(BF16)
        gq[hi, c] = (nn(b1, k[:, c]) + entering[hi]).astype(BF16)
        gks[lo, c] = tn(b0, q[lo, c]) + tn(b1[:, lo], q[hi, c])
        gks[hi, c] = tn(b1[:, hi], q[hi, c])
        w1 = wts[h, hi, :]
        out[lo, c] = tn(wts[h, lo, lo], grad[lo, c]) + tn(w1[:, lo], grad[hi, c])
        out[hi, c] = tn(w1[:, hi], grad[hi, c])

    def finish_b(h, low):
        c = cols(h)
        gk[:, c] = (gks[:, c] + nt(v[:, c] * mleave[...], low)).astype(BF16)
        gv[:, c] = (out[:, c] + nn(k[:, c] * mleave[...], low)).astype(BF16)

    slots(bwd, inside_b, finish_b)
    fwd.drain()
    bwd.drain()


def on_device(n, nh, queries, keys, values, gain, cotangent, doc_lengths):
    tokens, wide = queries.shape
    heads = wide // DH
    vmem = pl.BlockSpec(memory_space=pltpu.VMEM)
    state = pltpu.VMEM((heads, DH, DH), F32)
    sems = pltpu.SemaphoreType.DMA((heads,))
    low = pltpu.VMEM((tokens, DH), BF16)
    shape = jax.ShapeDtypeStruct((tokens, wide), BF16)
    return pl.pallas_call(
        functools.partial(kernel, n, nh, doc_lengths.shape[0]),
        out_shape=(shape,) * 4,
        in_specs=[pl.BlockSpec(memory_space=pltpu.SMEM)] + [vmem] * 5,
        out_specs=(vmem,) * 4,
        scratch_shapes=[
            pltpu.VMEM((heads, tokens, tokens), BF16),
            pltpu.VMEM((tokens, wide), F32),
            pltpu.VMEM((tokens, wide), F32),
            pltpu.VMEM((tokens, wide), BF16),
            pltpu.VMEM((heads, DH, DH), BF16),
            pltpu.VMEM((tokens, tokens), jnp.int32),
            low, low, low, low,
            pltpu.VMEM((2, tokens, DH), F32),
            pltpu.VMEM((nh - 1, 2, tokens, DH), F32),
        ]
        + [state] * 12
        + [sems] * 12
        + [pltpu.SemaphoreType.DMA((nh - 1,))] * 2,
        compiler_params=pltpu.CompilerParams(
            collective_id=0, has_side_effects=True, vmem_limit_bytes=60 * 1024 * 1024
        ),
    )(doc_lengths, queries, keys, values, gain.reshape(1, wide), cotangent)


def solution(mesh):
    placed = (
        P("seq", "head"),
        P("seq", "head"),
        P("seq", "head"),
        P("head"),
        P("seq", "head"),
        P(),
    )
    return jax.shard_map(
        functools.partial(on_device, mesh.shape["seq"], mesh.shape["head"]),
        mesh=mesh,
        in_specs=placed,
        out_specs=(P("seq", "head"), P("seq", "head"), P("seq", "head"), P("seq", "head")),
        check_vma=False,
    )
```

```python
import functools

import jax
import jax.numpy as jnp
from jax import lax
from jax.experimental import pallas as pl
from jax.experimental.pallas import tpu as pltpu
from jax.sharding import PartitionSpec as P

DH = 128
HEADS = 32
QUAD = 4
LAG = 3
HOP = 2

epsilon = 1e-05
MESH = pl.DeviceIdType.MESH
F32 = jnp.float32
BF16 = jnp.bfloat16


def nn(a, b):
    return lax.dot_general(a, b, (((1,), (0,)), ((), ())), preferred_element_type=F32)


def nt(a, b):
    return lax.dot_general(a, b, (((1,), (1,)), ((), ())), preferred_element_type=F32)


def tn(a, b):
    return lax.dot_general(a, b, (((0,), (0,)), ((), ())), preferred_element_type=F32)


def pick(flag, one, other):
    return jnp.where(flag, one, other).astype(F32)


def equal(a, b):
    return jnp.where(a == b, 1.0, 0.0).astype(F32)


def kernel(
    n, nh, docs,
    lens, qh, kh, vh, gain, coth,
    atth, gqh, gkh, gvh,
    q, k, v, cot, att, gq, gk, gv,
    wts, out, gks, grad, carr,
    vis, ment, mopen, mclose, mleave, part, peer,
    loc_f, pair_f, chain_f, rx_f, ry_f, rz_f,
    loc_b, pair_b, chain_b, rx_b, ry_b, rz_b,
    sx_f, sy_f, sz_f, tx_f, ty_f, tz_f,
    sx_b, sy_b, sz_b, tx_b, ty_b, tz_b,
    sh, th, sin, satt, sgq, sgk, sgv,
):
    load_q = pltpu.make_async_copy(qh, q, sin.at[0])
    load_k = pltpu.make_async_copy(kh, k, sin.at[1])
    load_v = pltpu.make_async_copy(vh, v, sin.at[2])
    load_cot = pltpu.make_async_copy(coth, cot, sin.at[3])
    load_k.start()
    load_v.start()
    load_q.start()
    load_cot.start()
    tokens = q.shape[0]
    half = tokens // 2
    heads = q.shape[1] // DH
    width = float(HEADS * DH)
    me = lax.axis_index("seq")
    mine = lax.axis_index("head")
    odd = lax.rem(me, 2)
    zc = lax.div(me, QUAD)
    nz = n // QUAD
    q0 = zc * QUAD
    upper = lax.div(me - q0, 2)
    pb = me - odd
    px = me + 1 - 2 * odd
    py = me + 2 - 4 * upper
    up = lax.rem(me + QUAD, n)
    down = lax.rem(me + n - QUAD, n)

    barrier = pltpu.get_barrier_semaphore()
    pl.semaphore_signal(barrier, inc=1, device_id={"seq": px}, device_id_type=MESH)
    pl.semaphore_signal(barrier, inc=1, device_id={"seq": py}, device_id_type=MESH)

    @pl.when(zc < nz - 1)
    def _():
        pl.semaphore_signal(barrier, inc=1, device_id={"seq": up}, device_id_type=MESH)

    @pl.when(zc > 0)
    def _():
        pl.semaphore_signal(barrier, inc=1, device_id={"seq": down}, device_id_type=MESH)

    for d in range(1, nh):
        pl.semaphore_signal(
            barrier, inc=1, device_id={"head": lax.rem(mine + d, nh)}, device_id_type=MESH
        )

    starts = []
    total = jnp.int32(0)
    for i in range(docs):
        starts.append(total)
        total = total + lens[i]

    def doc_of(p):
        count = jnp.int32(0)
        for s in starts:
            count = count + jnp.where(s <= p, 1, 0).astype(jnp.int32)
        return count

    before = {}
    after = {}
    for name, i in (("q0", q0), ("q2", q0 + 2), ("q4", q0 + 4), ("pb", pb), ("p1", pb + 1),
                    ("p2", pb + 2), ("me", me), ("m1", me + 1)):
        before[name] = doc_of(i * tokens - 1)
        after[name] = doc_of(i * tokens)

    anchor = me * tokens
    pos_c = lax.broadcasted_iota(jnp.int32, (tokens, DH), 0) + anchor
    doc_c = jnp.zeros((tokens, DH), jnp.int32)
    for s in starts:
        doc_c = doc_c + jnp.where(pos_c >= s, 1, 0)
    ment[...] = jnp.where(doc_c == before["me"], 1.0, 0.0).astype(BF16)
    mopen[...] = jnp.where(doc_c == after["me"], 1.0, 0.0).astype(BF16)
    mclose[...] = jnp.where(doc_c == before["m1"], 1.0, 0.0).astype(BF16)
    mleave[...] = jnp.where(doc_c == after["m1"], 1.0, 0.0).astype(BF16)

    pl.semaphore_wait(
        barrier,
        2 + nh - 1
        + jnp.where(zc < nz - 1, 1, 0).astype(jnp.int32)
        + jnp.where(zc > 0, 1, 0).astype(jnp.int32),
    )

    def cols(h):
        return pl.ds(pl.multiple_of(h * DH, DH), DH)

    def store(src, dst, sem, h):
        c = cols(h)
        return pltpu.make_async_copy(src.at[:, c], dst.at[:, c], sem.at[h])

    def send(src, dst, ss, rs, h, to):
        return pltpu.make_async_remote_copy(
            src_ref=src.at[h], dst_ref=dst.at[h], send_sem=ss.at[h], recv_sem=rs.at[h],
            device_id={"seq": to}, device_id_type=MESH,
        )

    class Scan:
        def __init__(self, bufs, sems, to, place, coef):
            self.loc, self.pair, self.chain, self.rx, self.ry, self.rz = bufs
            self.sx, self.sy, self.sz, self.tx, self.ty, self.tz = sems
            self.to, self.place = to, place
            self.al, self.ar, self.er, self.bl, self.br, self.e2, self.kq, self.e3 = coef

        def cx(self, h):
            return send(self.loc, self.rx, self.sx, self.tx, h, px)

        def cy(self, h):
            return send(self.pair, self.ry, self.sy, self.ty, h, py)

        def cz(self, h):
            return send(self.chain, self.rz, self.sz, self.tz, h, self.to)

        def clear(self):
            @pl.when(self.place == 0)
            def _():
                self.rz[...] = jnp.zeros_like(self.rz)

        def xstage(self, h):
            self.cx(h).wait_recv()
            self.pair[h] = self.al * self.loc[h] + self.ar * self.rx[h]
            self.cy(h).start()

        def ystage(self, h):
            self.cy(h).wait_recv()

            @pl.when(self.place == 0)
            def _():
                self.chain[h] = self.bl * self.pair[h] + self.br * self.ry[h]
                self.cz(h).start()

        def zstage(self, h):
            @pl.when(self.place > 0)
            def _():
                self.cz(h).wait_recv()

            @pl.when((self.place > 0) & (self.place < nz - 1))
            def _():
                total = self.bl * self.pair[h] + self.br * self.ry[h]
                self.chain[h] = total + self.kq * self.rz[h]
                self.cz(h).start()

            return self.er * self.rx[h] + self.e2 * self.ry[h] + self.e3 * self.rz[h]

        def drain(self):
            def body(h, carry):
                self.cx(h).wait_send()
                self.cy(h).wait_send()

                @pl.when(self.place < nz - 1)
                def _():
                    self.cz(h).wait_send()

                return carry

            lax.fori_loop(0, heads, body, 0)

    is_odd, is_upper = odd == 1, upper == 1
    kx = equal(before["p1"], before["p2"])
    ky = equal(before["q2"], before["q4"])
    fwd = Scan(
        (loc_f, pair_f, chain_f, rx_f, ry_f, rz_f),
        (sx_f, sy_f, sz_f, tx_f, ty_f, tz_f),
        up, zc,
        (pick(is_odd, 1.0, kx), pick(is_odd, kx, 1.0), pick(is_odd, 1.0, 0.0),
         pick(is_upper, 1.0, ky), pick(is_upper, ky, 1.0),
         pick(is_upper, equal(before["pb"], before["me"]), 0.0),
         equal(before["q0"], before["q4"]), equal(before["q0"], before["me"])),
    )
    kx = equal(after["pb"], after["p1"])
    ky = equal(after["q0"], after["q2"])
    bwd = Scan(
        (loc_b, pair_b, chain_b, rx_b, ry_b, rz_b),
        (sx_b, sy_b, sz_b, tx_b, ty_b, tz_b),
        down, nz - 1 - zc,
        (pick(is_odd, kx, 1.0), pick(is_odd, 1.0, kx), pick(is_odd, 0.0, 1.0),
         pick(is_upper, ky, 1.0), pick(is_upper, 1.0, ky),
         pick(is_upper, 0.0, equal(after["m1"], after["p2"])),
         equal(after["q0"], after["q4"]), equal(after["m1"], after["q4"])),
    )

    def slots(scan, inside, finish):
        def place_of(s):
            return s - LAG - HOP * scan.place

        def chain_step(s):
            h = place_of(s)

            @pl.when((h >= 0) & (h < heads))
            def _():
                finish(h, scan.zstage(h).astype(BF16))

        def main(s, carry):
            scan.xstage(s)

            @pl.when(s >= LAG)
            def _():
                scan.ystage(s - LAG)

            inside(s)
            chain_step(s)
            return carry

        lax.fori_loop(0, heads, main, 0)

        def tail(s, carry):
            @pl.when(s < heads + LAG)
            def _():
                scan.ystage(s - LAG)

            chain_step(s)
            return carry

        lax.fori_loop(heads, heads + LAG + HOP * (nz - 1), tail, 0)

    load_k.wait()
    load_v.wait()

    def first(h, carry):
        c = cols(h)
        loc_f[h] = tn(k[:, c] * mclose[...], v[:, c])
        fwd.cx(h).start()
        return carry

    lax.fori_loop(0, heads, first, 0)
    fwd.clear()
    bwd.clear()

    pos_r = lax.broadcasted_iota(jnp.int32, (8, tokens), 1) + anchor
    doc_r = jnp.zeros((8, tokens), jnp.int32)
    for s in starts:
        doc_r = doc_r + jnp.where(pos_r >= s, 1, 0)
    row = lax.broadcasted_iota(jnp.int32, (tokens, tokens), 0)
    col = lax.broadcasted_iota(jnp.int32, (tokens, tokens), 1)
    vis[...] = jnp.where((doc_c[:, :1] == doc_r[:1, :]) & (row >= col), 1, 0)
    part[...] = jnp.zeros_like(part)

    lo, hi = slice(0, half), slice(half, tokens)

    def masked(scores, rows, columns):
        return jnp.where(vis[rows, columns] != 0, scores, 0.0).astype(BF16)

    def inside_f(h):
        c = cols(h)
        w0 = masked(nt(q[lo, c], k[lo, c]), lo, lo)
        w1 = masked(nt(q[hi, c], k[:, c]), hi, slice(0, tokens))
        wts[h, lo, lo] = w0
        wts[h, hi, :] = w1
        out[lo, c] = nn(w0, v[lo, c])
        out[hi, c] = nn(w1, v[:, c])

    def finish_f(h, low):
        c = cols(h)
        carr[h] = low
        o = out[:, c] + nn(q[:, c] * ment[...], low)
        out[:, c] = o
        part[0] += o * o
        part[1] += (cot[:, c].astype(F32) * gain[:, c]) * o

    load_q.wait()
    load_cot.wait()
    slots(fwd, inside_f, finish_f)

    def swap(d):
        return pltpu.make_async_remote_copy(
            src_ref=part, dst_ref=peer.at[d - 1], send_sem=sh.at[d - 1], recv_sem=th.at[d - 1],
            device_id={"head": lax.rem(mine + d, nh)}, device_id_type=MESH,
        )

    for d in range(1, nh):
        swap(d).start()
    for d in range(1, nh):
        swap(d).wait_recv()
    squares, cross = part[0], part[1]
    for d in range(1, nh):
        squares = squares + peer[d - 1, 0]
        cross = cross + peer[d - 1, 1]
    for d in range(1, nh):
        swap(d).wait_send()
    root = jnp.sqrt(jnp.sum(squares, axis=1, keepdims=True) / width + epsilon)
    coef = jnp.sum(cross, axis=1, keepdims=True) / (width * root * root)
    part[0] = jnp.broadcast_to(1.0 / root, (tokens, DH))
    part[1] = jnp.broadcast_to(coef, (tokens, DH))

    def middle(h, carry):
        c = cols(h)
        o = out[:, c]
        inv = part[0]
        gn = gain[:, c]
        att[:, c] = (o * inv * gn).astype(BF16)
        store(att, atth, satt, h).start()
        g = ((cot[:, c].astype(F32) * gn - o * part[1]) * inv).astype(BF16)
        grad[:, c] = g
        loc_b[h] = tn(q[:, c] * mopen[...], g)
        bwd.cx(h).start()
        return carry

    lax.fori_loop(0, heads, middle, 0)

    def inside_b(h):
        c = cols(h)
        b0 = masked(nt(grad[lo, c], v[lo, c]), lo, lo)
        b1 = masked(nt(grad[hi, c], v[:, c]), hi, slice(0, tokens))
        entering = nt(grad[:, c] * ment[...], carr[h])
        gq[lo, c] = (nn(b0, k[lo, c]) + entering[lo]).astype(BF16)
        gq[hi, c] = (nn(b1, k[:, c]) + entering[hi]).astype(BF16)
        store(gq, gqh, sgq, h).start()
        gks[lo, c] = tn(b0, q[lo, c]) + tn(b1[:, lo], q[hi, c])
        gks[hi, c] = tn(b1[:, hi], q[hi, c])
        w1 = wts[h, hi, :]
        out[lo, c] = tn(wts[h, lo, lo], grad[lo, c]) + tn(w1[:, lo], grad[hi, c])
        out[hi, c] = tn(w1[:, hi], grad[hi, c])

    def finish_b(h, low):
        c = cols(h)
        gk[:, c] = (gks[:, c] + nt(v[:, c] * mleave[...], low)).astype(BF16)
        gv[:, c] = (out[:, c] + nn(k[:, c] * mleave[...], low)).astype(BF16)
        store(gk, gkh, sgk, h).start()
        store(gv, gvh, sgv, h).start()

    slots(bwd, inside_b, finish_b)
    fwd.drain()
    bwd.drain()

    def flush(h, carry):
        store(att, atth, satt, h).wait()
        store(gq, gqh, sgq, h).wait()
        store(gk, gkh, sgk, h).wait()
        store(gv, gvh, sgv, h).wait()
        return carry

    lax.fori_loop(0, heads, flush, 0)


def move(*refs):
    for src, dst in zip(refs[:4], refs[4:]):
        dst[...] = src[...]


def on_device(n, nh, queries, keys, values, gain, cotangent, doc_lengths):
    tokens, wide = queries.shape
    heads = wide // DH
    vmem = pl.BlockSpec(memory_space=pltpu.VMEM)
    hbm = pl.BlockSpec(memory_space=pl.ANY)
    block = pl.BlockSpec((tokens // 8, wide), lambda i: (i, 0))
    state = pltpu.VMEM((heads, DH, DH), F32)
    sems = pltpu.SemaphoreType.DMA((heads,))
    low = pltpu.VMEM((tokens, DH), BF16)
    shape = jax.ShapeDtypeStruct((tokens, wide), BF16)
    results = pl.pallas_call(
        functools.partial(kernel, n, nh, doc_lengths.shape[0]),
        out_shape=(shape,) * 4,
        in_specs=[pl.BlockSpec(memory_space=pltpu.SMEM)] + [hbm] * 3 + [vmem, hbm],
        out_specs=(hbm,) * 4,
        scratch_shapes=[pltpu.VMEM((tokens, wide), BF16)] * 8
        + [
            pltpu.VMEM((heads, tokens, tokens), BF16),
            pltpu.VMEM((tokens, wide), F32),
            pltpu.VMEM((tokens, wide), F32),
            pltpu.VMEM((tokens, wide), BF16),
            pltpu.VMEM((heads, DH, DH), BF16),
            pltpu.VMEM((tokens, tokens), jnp.int32),
            low, low, low, low,
            pltpu.VMEM((2, tokens, DH), F32),
            pltpu.VMEM((nh - 1, 2, tokens, DH), F32),
        ]
        + [state] * 12
        + [sems] * 12
        + [pltpu.SemaphoreType.DMA((nh - 1,))] * 2
        + [pltpu.SemaphoreType.DMA((4,))]
        + [sems] * 4,
        compiler_params=pltpu.CompilerParams(
            collective_id=0, has_side_effects=True, vmem_limit_bytes=60 * 1024 * 1024
        ),
    )(doc_lengths, queries, keys, values, gain.reshape(1, wide), cotangent)
    return pl.pallas_call(
        move,
        grid=(8,),
        out_shape=(shape,) * 4,
        in_specs=[block] * 4,
        out_specs=(block,) * 4,
    )(*results)


def solution(mesh):
    placed = (
        P("seq", "head"),
        P("seq", "head"),
        P("seq", "head"),
        P("head"),
        P("seq", "head"),
        P(),
    )
    return jax.shard_map(
        functools.partial(on_device, mesh.shape["seq"], mesh.shape["head"]),
        mesh=mesh,
        in_specs=placed,
        out_specs=(P("seq", "head"), P("seq", "head"), P("seq", "head"), P("seq", "head")),
        check_vma=False,
    )
```

```python
import functools

import jax
import jax.numpy as jnp
from jax import lax
from jax.experimental import pallas as pl
from jax.experimental.pallas import tpu as pltpu
from jax.sharding import PartitionSpec as P

DH = 128
HEADS = 32
QUAD = 4
LAG = 3
HOP = 2

epsilon = 1e-05
MESH = pl.DeviceIdType.MESH
F32 = jnp.float32
BF16 = jnp.bfloat16


def nn(a, b):
    return lax.dot_general(a, b, (((1,), (0,)), ((), ())), preferred_element_type=F32)


def nt(a, b):
    return lax.dot_general(a, b, (((1,), (1,)), ((), ())), preferred_element_type=F32)


def tn(a, b):
    return lax.dot_general(a, b, (((0,), (0,)), ((), ())), preferred_element_type=F32)


def pick(flag, one, other):
    return jnp.where(flag, one, other).astype(F32)


def equal(a, b):
    return jnp.where(a == b, 1.0, 0.0).astype(F32)


def kernel(
    n, nh, docs,
    lens, qh, kh, vh, gain, coth,
    atth, gqh, gkh, gvh,
    q, k, v, cot, att, gq, gk, gv,
    wts, out, gks, grad, carr,
    vis, ment, mopen, mclose, mleave, part, peer,
    loc_f, pair_f, chain_f, rx_f, ry_f, rz_f,
    loc_b, pair_b, chain_b, rx_b, ry_b, rz_b,
    sx_f, sy_f, sz_f, tx_f, ty_f, tz_f,
    sx_b, sy_b, sz_b, tx_b, ty_b, tz_b,
    sh, th, sin, satt, sgq, sgk, sgv,
):
    load_q = pltpu.make_async_copy(qh, q, sin.at[0])
    load_k = pltpu.make_async_copy(kh, k, sin.at[1])
    load_v = pltpu.make_async_copy(vh, v, sin.at[2])
    load_cot = pltpu.make_async_copy(coth, cot, sin.at[3])
    load_k.start()
    load_v.start()
    load_q.start()
    load_cot.start()
    tokens = q.shape[0]
    half = tokens // 2
    heads = q.shape[1] // DH
    width = float(HEADS * DH)
    me = lax.axis_index("seq")
    mine = lax.axis_index("head")
    odd = lax.rem(me, 2)
    zc = lax.div(me, QUAD)
    nz = n // QUAD
    q0 = zc * QUAD
    upper = lax.div(me - q0, 2)
    pb = me - odd
    px = me + 1 - 2 * odd
    py = me + 2 - 4 * upper
    up = lax.rem(me + QUAD, n)
    down = lax.rem(me + n - QUAD, n)

    barrier = pltpu.get_barrier_semaphore()
    pl.semaphore_signal(barrier, inc=1, device_id={"seq": px}, device_id_type=MESH)
    pl.semaphore_signal(barrier, inc=1, device_id={"seq": py}, device_id_type=MESH)

    @pl.when(zc < nz - 1)
    def _():
        pl.semaphore_signal(barrier, inc=1, device_id={"seq": up}, device_id_type=MESH)

    @pl.when(zc > 0)
    def _():
        pl.semaphore_signal(barrier, inc=1, device_id={"seq": down}, device_id_type=MESH)

    for d in range(1, nh):
        pl.semaphore_signal(
            barrier, inc=1, device_id={"head": lax.rem(mine + d, nh)}, device_id_type=MESH
        )

    starts = []
    total = jnp.int32(0)
    for i in range(docs):
        starts.append(total)
        total = total + lens[i]

    def doc_of(p):
        count = jnp.int32(0)
        for s in starts:
            count = count + jnp.where(s <= p, 1, 0).astype(jnp.int32)
        return count

    before = {}
    after = {}
    for name, i in (("q0", q0), ("q2", q0 + 2), ("q4", q0 + 4), ("pb", pb), ("p1", pb + 1),
                    ("p2", pb + 2), ("me", me), ("m1", me + 1)):
        before[name] = doc_of(i * tokens - 1)
        after[name] = doc_of(i * tokens)

    anchor = me * tokens
    pos_c = lax.broadcasted_iota(jnp.int32, (tokens, DH), 0) + anchor
    doc_c = jnp.zeros((tokens, DH), jnp.int32)
    for s in starts:
        doc_c = doc_c + jnp.where(pos_c >= s, 1, 0)
    ment[...] = jnp.where(doc_c == before["me"], 1.0, 0.0).astype(BF16)
    mopen[...] = jnp.where(doc_c == after["me"], 1.0, 0.0).astype(BF16)
    mclose[...] = jnp.where(doc_c == before["m1"], 1.0, 0.0).astype(BF16)
    mleave[...] = jnp.where(doc_c == after["m1"], 1.0, 0.0).astype(BF16)

    pl.semaphore_wait(
        barrier,
        2 + nh - 1
        + jnp.where(zc < nz - 1, 1, 0).astype(jnp.int32)
        + jnp.where(zc > 0, 1, 0).astype(jnp.int32),
    )

    def cols(h):
        return pl.ds(pl.multiple_of(h * DH, DH), DH)

    def store(src, dst, sem, h):
        c = cols(h)
        return pltpu.make_async_copy(src.at[:, c], dst.at[:, c], sem.at[h])

    def send(src, dst, ss, rs, h, to):
        return pltpu.make_async_remote_copy(
            src_ref=src.at[h], dst_ref=dst.at[h], send_sem=ss.at[h], recv_sem=rs.at[h],
            device_id={"seq": to}, device_id_type=MESH,
        )

    class Scan:
        def __init__(self, bufs, sems, to, place, coef):
            self.loc, self.pair, self.chain, self.rx, self.ry, self.rz = bufs
            self.sx, self.sy, self.sz, self.tx, self.ty, self.tz = sems
            self.to, self.place = to, place
            self.al, self.ar, self.er, self.bl, self.br, self.e2, self.kq, self.e3 = coef

        def cx(self, h):
            return send(self.loc, self.rx, self.sx, self.tx, h, px)

        def cy(self, h):
            return send(self.pair, self.ry, self.sy, self.ty, h, py)

        def cz(self, h):
            return send(self.chain, self.rz, self.sz, self.tz, h, self.to)

        def clear(self):
            @pl.when(self.place == 0)
            def _():
                self.rz[...] = jnp.zeros_like(self.rz)

        def xstage(self, h):
            self.cx(h).wait_recv()
            self.pair[h] = self.al * self.loc[h] + self.ar * self.rx[h]
            self.cy(h).start()

        def ystage(self, h):
            self.cy(h).wait_recv()

            @pl.when(self.place == 0)
            def _():
                self.chain[h] = self.bl * self.pair[h] + self.br * self.ry[h]
                self.cz(h).start()

        def zstage(self, h):
            @pl.when(self.place > 0)
            def _():
                self.cz(h).wait_recv()

            @pl.when((self.place > 0) & (self.place < nz - 1))
            def _():
                total = self.bl * self.pair[h] + self.br * self.ry[h]
                self.chain[h] = total + self.kq * self.rz[h]
                self.cz(h).start()

            return self.er * self.rx[h] + self.e2 * self.ry[h] + self.e3 * self.rz[h]

        def drain(self):
            def body(h, carry):
                self.cx(h).wait_send()
                self.cy(h).wait_send()

                @pl.when(self.place < nz - 1)
                def _():
                    self.cz(h).wait_send()

                return carry

            lax.fori_loop(0, heads, body, 0)

    is_odd, is_upper = odd == 1, upper == 1
    kx = equal(before["p1"], before["p2"])
    ky = equal(before["q2"], before["q4"])
    fwd = Scan(
        (loc_f, pair_f, chain_f, rx_f, ry_f, rz_f),
        (sx_f, sy_f, sz_f, tx_f, ty_f, tz_f),
        up, zc,
        (pick(is_odd, 1.0, kx), pick(is_odd, kx, 1.0), pick(is_odd, 1.0, 0.0),
         pick(is_upper, 1.0, ky), pick(is_upper, ky, 1.0),
         pick(is_upper, equal(before["pb"], before["me"]), 0.0),
         equal(before["q0"], before["q4"]), equal(before["q0"], before["me"])),
    )
    kx = equal(after["pb"], after["p1"])
    ky = equal(after["q0"], after["q2"])
    bwd = Scan(
        (loc_b, pair_b, chain_b, rx_b, ry_b, rz_b),
        (sx_b, sy_b, sz_b, tx_b, ty_b, tz_b),
        down, nz - 1 - zc,
        (pick(is_odd, kx, 1.0), pick(is_odd, 1.0, kx), pick(is_odd, 0.0, 1.0),
         pick(is_upper, ky, 1.0), pick(is_upper, 1.0, ky),
         pick(is_upper, 0.0, equal(after["m1"], after["p2"])),
         equal(after["q0"], after["q4"]), equal(after["m1"], after["q4"])),
    )

    def slots(scan, inside, finish):
        def place_of(s):
            return s - LAG - HOP * scan.place

        def chain_step(s):
            h = place_of(s)

            @pl.when((h >= 0) & (h < heads))
            def _():
                finish(h, scan.zstage(h).astype(BF16))

        def main(s, carry):
            scan.xstage(s)

            @pl.when(s >= LAG)
            def _():
                scan.ystage(s - LAG)

            inside(s)
            chain_step(s)
            return carry

        lax.fori_loop(0, heads, main, 0)

        def tail(s, carry):
            @pl.when(s < heads + LAG)
            def _():
                scan.ystage(s - LAG)

            chain_step(s)
            return carry

        lax.fori_loop(heads, heads + LAG + HOP * (nz - 1), tail, 0)

    load_k.wait()
    load_v.wait()

    def first(h, carry):
        c = cols(h)
        loc_f[h] = tn(k[:, c] * mclose[...], v[:, c])
        fwd.cx(h).start()
        return carry

    lax.fori_loop(0, heads, first, 0)
    fwd.clear()
    bwd.clear()

    pos_r = lax.broadcasted_iota(jnp.int32, (8, tokens), 1) + anchor
    doc_r = jnp.zeros((8, tokens), jnp.int32)
    for s in starts:
        doc_r = doc_r + jnp.where(pos_r >= s, 1, 0)
    row = lax.broadcasted_iota(jnp.int32, (tokens, tokens), 0)
    col = lax.broadcasted_iota(jnp.int32, (tokens, tokens), 1)
    vis[...] = jnp.where((doc_c[:, :1] == doc_r[:1, :]) & (row >= col), 1, 0)
    part[...] = jnp.zeros_like(part)

    lo, hi = slice(0, half), slice(half, tokens)

    def masked(scores, rows, columns):
        return jnp.where(vis[rows, columns] != 0, scores, 0.0).astype(BF16)

    def inside_f(h):
        c = cols(h)
        w0 = masked(nt(q[lo, c], k[lo, c]), lo, lo)
        w1 = masked(nt(q[hi, c], k[:, c]), hi, slice(0, tokens))
        wts[h, lo, lo] = w0
        wts[h, hi, :] = w1
        out[lo, c] = nn(w0, v[lo, c])
        out[hi, c] = nn(w1, v[:, c])

    def finish_f(h, low):
        c = cols(h)
        carr[h] = low
        o = out[:, c] + nn(q[:, c] * ment[...], low)
        out[:, c] = o
        part[0] += o * o
        part[1] += (cot[:, c].astype(F32) * gain[:, c]) * o

    load_q.wait()
    load_cot.wait()
    slots(fwd, inside_f, finish_f)

    def swap(d):
        return pltpu.make_async_remote_copy(
            src_ref=part, dst_ref=peer.at[d - 1], send_sem=sh.at[d - 1], recv_sem=th.at[d - 1],
            device_id={"head": lax.rem(mine + d, nh)}, device_id_type=MESH,
        )

    for d in range(1, nh):
        swap(d).start()
    for d in range(1, nh):
        swap(d).wait_recv()
    squares, cross = part[0], part[1]
    for d in range(1, nh):
        squares = squares + peer[d - 1, 0]
        cross = cross + peer[d - 1, 1]
    for d in range(1, nh):
        swap(d).wait_send()
    root = jnp.sqrt(jnp.sum(squares, axis=1, keepdims=True) / width + epsilon)
    coef = jnp.sum(cross, axis=1, keepdims=True) / (width * root * root)
    part[0] = jnp.broadcast_to(1.0 / root, (tokens, DH))
    part[1] = jnp.broadcast_to(coef, (tokens, DH))

    def middle(h, carry):
        c = cols(h)
        o = out[:, c]
        inv = part[0]
        gn = gain[:, c]
        att[:, c] = (o * inv * gn).astype(BF16)
        store(att, atth, satt, h).start()
        g = ((cot[:, c].astype(F32) * gn - o * part[1]) * inv).astype(BF16)
        grad[:, c] = g
        loc_b[h] = tn(q[:, c] * mopen[...], g)
        bwd.cx(h).start()
        return carry

    lax.fori_loop(0, heads, middle, 0)

    def inside_b(h):
        c = cols(h)
        b0 = masked(nt(grad[lo, c], v[lo, c]), lo, lo)
        b1 = masked(nt(grad[hi, c], v[:, c]), hi, slice(0, tokens))
        entering = nt(grad[:, c] * ment[...], carr[h])
        gq[lo, c] = (nn(b0, k[lo, c]) + entering[lo]).astype(BF16)
        gq[hi, c] = (nn(b1, k[:, c]) + entering[hi]).astype(BF16)
        store(gq, gqh, sgq, h).start()
        gks[lo, c] = tn(b0, q[lo, c]) + tn(b1[:, lo], q[hi, c])
        gks[hi, c] = tn(b1[:, hi], q[hi, c])
        w1 = wts[h, hi, :]
        out[lo, c] = tn(wts[h, lo, lo], grad[lo, c]) + tn(w1[:, lo], grad[hi, c])
        out[hi, c] = tn(w1[:, hi], grad[hi, c])

    def finish_b(h, low):
        c = cols(h)
        gk[:, c] = (gks[:, c] + nt(v[:, c] * mleave[...], low)).astype(BF16)
        gv[:, c] = (out[:, c] + nn(k[:, c] * mleave[...], low)).astype(BF16)
        store(gk, gkh, sgk, h).start()
        store(gv, gvh, sgv, h).start()

    slots(bwd, inside_b, finish_b)
    fwd.drain()
    bwd.drain()

    def flush(h, carry):
        store(att, atth, satt, h).wait()
        store(gq, gqh, sgq, h).wait()
        store(gk, gkh, sgk, h).wait()
        store(gv, gvh, sgv, h).wait()
        return carry

    lax.fori_loop(0, heads, flush, 0)


def on_device(n, nh, queries, keys, values, gain, cotangent, doc_lengths):
    tokens, wide = queries.shape
    heads = wide // DH
    vmem = pl.BlockSpec(memory_space=pltpu.VMEM)
    hbm = pl.BlockSpec(memory_space=pl.ANY)
    state = pltpu.VMEM((heads, DH, DH), F32)
    sems = pltpu.SemaphoreType.DMA((heads,))
    low = pltpu.VMEM((tokens, DH), BF16)
    shape = jax.ShapeDtypeStruct((tokens, wide), BF16)
    results = pl.pallas_call(
        functools.partial(kernel, n, nh, doc_lengths.shape[0]),
        out_shape=(pltpu.VMEM((tokens, wide), BF16),) * 4,
        in_specs=[pl.BlockSpec(memory_space=pltpu.SMEM)] + [hbm] * 3 + [vmem, hbm],
        out_specs=(hbm,) * 4,
        scratch_shapes=[pltpu.VMEM((tokens, wide), BF16)] * 8
        + [
            pltpu.VMEM((heads, tokens, tokens), BF16),
            pltpu.VMEM((tokens, wide), F32),
            pltpu.VMEM((tokens, wide), F32),
            pltpu.VMEM((tokens, wide), BF16),
            pltpu.VMEM((heads, DH, DH), BF16),
            pltpu.VMEM((tokens, tokens), jnp.int32),
            low, low, low, low,
            pltpu.VMEM((2, tokens, DH), F32),
            pltpu.VMEM((nh - 1, 2, tokens, DH), F32),
        ]
        + [state] * 12
        + [sems] * 12
        + [pltpu.SemaphoreType.DMA((nh - 1,))] * 2
        + [pltpu.SemaphoreType.DMA((4,))]
        + [sems] * 4,
        compiler_params=pltpu.CompilerParams(
            collective_id=0, has_side_effects=True, vmem_limit_bytes=51 * 1024 * 1024
        ),
    )(doc_lengths, queries, keys, values, gain.reshape(1, wide), cotangent)
    return results


def solution(mesh):
    placed = (
        P("seq", "head"),
        P("seq", "head"),
        P("seq", "head"),
        P("head"),
        P("seq", "head"),
        P(),
    )
    return jax.shard_map(
        functools.partial(on_device, mesh.shape["seq"], mesh.shape["head"]),
        mesh=mesh,
        in_specs=placed,
        out_specs=(P("seq", "head"), P("seq", "head"), P("seq", "head"), P("seq", "head")),
        check_vma=False,
    )
```
